32 devices in a mesh: parts: 2 (over y), dp: 4 (over x, core), tensor: 4 (over z).
Axes of the slice: x: 2, y: 2, z: 4, core: 2. Of those that a mesh axis runs over, the one named last changes fastest.
Arguments:
- gate_preact: bfloat16 [3072, 28672], P(('parts', 'dp'), 'tensor'), parts along dimension 0, may hold values from -6 to 6
- up_output: bfloat16 [3072, 28672], P(('parts', 'dp'), 'tensor'), parts along dimension 0, may hold values from -6 to 6
- normed_input: bfloat16 [3072, 8192], P(('parts', 'dp'), 'tensor'), parts along dimension 0, may hold values from -6 to 6
- output_grad: bfloat16 [3072, 8192], P(('parts', 'dp'), 'tensor'), parts along dimension 0, may hold values from -6 to 6
- down_weight: bfloat16 [28672, 8192], P('tensor', 'dp'), may hold values from -0.0625 to 0.0625
- normed_basis: bfloat16 [8192, 64], P('tensor'), may hold values from -0.0625 to 0.0625
- output_basis: bfloat16 [8192, 64], P('tensor'), may hold values from -0.0625 to 0.0625
- hidden_basis: bfloat16 [28672, 64], P('tensor'), may hold values from -0.03125 to 0.03125
- up_basis: bfloat16 [28672, 64], P('tensor'), may hold values from -0.03125 to 0.03125
- val_bank: bfloat16 [16, 8192], P('tensor', 'dp'), may hold values from -6 to 6
- lengths: int32 [8, 6], P(('parts', 'dp')), parts along dimension 0, may hold values from 1 to 192, 384 in all within a row
Outputs:
- scores: float32 [48, 16], P(('parts', 'dp'), 'tensor'), parts along dimension 0
The draws below stay inside these ranges and needn't reach their ends.
There are 2 independent parts, one for each index of `parts`. The reference program is written for one: setup_inputs(seed, part) draws one part's arguments, and reference() takes and returns one part's arrays. A program takes and returns all parts, laid end to end along the dimension named above; an argument that names none is the same for every part. Nothing has to cross between parts.
Inputs may be any that keep to these rules, and one draw needn't show every extreme that they name: Each row holds the lengths of the 6 examples packed in order into the 384 tokens of one data group; a row sums to 384 and its longest example has exactly 192 tokens.
All inputs are finite; a program needn't handle non-finite values.
Results may differ from the reference program's by a relative error of at most 0.0041.
Values may be sent and summed in bfloat16 or wider, within the bound.
No kernel may reach another device: no remote copies, remote signals or barrier semaphores. Data moves between devices by JAX's collectives and lax.ppermute only.
A program may use at most 320 MiB of HBM per device.

```python
import math
from functools import partial
import jax
import jax.numpy as jnp
import numpy as np
from jax import lax

D = 8192
FF = 28672
R = 64
TOK = 384
EX = 6
MAXLEN = 192
GROUPS = 4
TOKENS = 1536
EXAMPLES = 24
VAL = 16


def shard_levels(stream_key, dims, pieces, smallest, high):
    gain, own = 1.0, jax.random.fold_in(stream_key, 6)
    for axis_at, blocks in pieces:
        heights = jnp.exp(jax.random.uniform(jax.random.fold_in(own, axis_at), (blocks,), jnp.float32, smallest / len(pieces), high / len(pieces)))
        gain = gain * jnp.repeat(heights, dims[axis_at] // blocks).reshape([-1 if axis == axis_at else 1 for axis in range(len(dims))])
    return gain


def split_up(count, total, bound, skew):
    loads = [(1 << 20) // math.isqrt(rank ** skew) + 1 for rank in range(2, count + 1)]
    rest, counts = total - bound - (count - 1), [1] * (count - 1)
    while rest > 0:
        candidates = [i for i in range(count - 1) if counts[i] < bound]
        pool, remaining = sum([loads[i] for i in candidates]), rest
        for i in candidates:
            extra = min(bound - counts[i], max(1, remaining * loads[i] // pool), rest)
            counts[i] = counts[i] + extra
            rest = rest - extra
    return np.array([bound] + counts)


def uneven_parts(key, number_of, total, reach, lean):
    if number_of == 2:
        one = jax.random.randint(key, (), max(1, total - reach), min(reach, total - 1) + 1)
        return jnp.stack([one, total - one])
    sizes = jnp.asarray(split_up(number_of, total, reach, lean), jnp.int32)
    twos = (number_of - 1) // 2
    source_of, sink = sizes[1:1 + 2 * twos:2], sizes[2:2 + 2 * twos:2]
    margin = jnp.minimum(source_of - 1, reach - sink)
    moved = jax.random.randint(jax.random.fold_in(key, 1), (twos,), 0, 1 << 20) % (margin + 1)
    sizes = sizes.at[1:1 + 2 * twos:2].set(source_of - moved).at[2:2 + 2 * twos:2].set(sink + moved)
    return sizes[jax.random.permutation(jax.random.fold_in(key, 2), number_of)]


def gaussian(rng, shape, deviation, bound, cuts=(), kind=jnp.bfloat16):
    values = deviation * jax.random.normal(rng, shape, jnp.float32)
    if cuts:
        values = values * shard_levels(rng, shape, cuts, -0.22, 0.18)
    return jnp.clip(values, -bound, bound).astype(kind)


def setup_inputs(seed: int = 0, part: int = 0) -> dict:
    arg_keys = jax.random.split(jax.random.key(seed), 12)
    part_keys = jax.random.split(jax.random.fold_in(arg_keys[11], part), 12)
    gate_preact = gaussian(part_keys[0], (TOKENS, FF), 1.0, 6.0, ((0, 4), (1, 4)))
    up_output = gaussian(part_keys[1], (TOKENS, FF), 1.0, 6.0, ((0, 4), (1, 4)))
    normed_input = gaussian(part_keys[2], (TOKENS, D), 1.0, 6.0, ((0, 4), (1, 4)))
    output_grad = gaussian(part_keys[3], (TOKENS, D), 1.0, 6.0, ((0, 4), (1, 4)))
    down_weight = gaussian(arg_keys[4], (FF, D), D ** -0.5, 0.0625, ((0, 4), (1, 4)))
    normed_basis = gaussian(arg_keys[5], (D, R), D ** -0.5, 0.0625, ((0, 4),))
    output_basis = gaussian(arg_keys[6], (D, R), D ** -0.5, 0.0625, ((0, 4),))
    hidden_basis = gaussian(arg_keys[7], (FF, R), FF ** -0.5, 0.03125, ((0, 4),))
    up_basis = gaussian(arg_keys[8], (FF, R), FF ** -0.5, 0.03125, ((0, 4),))
    val_bank = gaussian(arg_keys[9], (VAL, 2 * R * R), 1.0, 6.0, ((0, 4), (1, 4)))
    lengths = jax.vmap(lambda own: uneven_parts(own, EX, TOK, MAXLEN, 2))(jax.random.split(part_keys[10], GROUPS)).reshape((GROUPS, EX)).astype(jnp.int32)
    return dict(gate_preact=gate_preact, up_output=up_output, normed_input=normed_input, output_grad=output_grad, down_weight=down_weight, normed_basis=normed_basis, output_basis=output_basis, hidden_basis=hidden_basis, up_basis=up_basis, val_bank=val_bank, lengths=lengths)


def segment_matrix(token_count, lengths_row):
    seg_ends = jnp.cumsum(lengths_row).astype(jnp.int32)
    seg_starts = seg_ends - lengths_row.astype(jnp.int32)
    positions = jnp.arange(token_count, dtype=jnp.int32)
    inside = (positions[:, None] >= seg_starts[None, :]) & (positions[:, None] < seg_ends[None, :])
    return inside.astype(jnp.float32)

def reference(gate_preact, up_output, normed_input, output_grad, down_weight, normed_basis, output_basis, hidden_basis, up_basis, val_bank, lengths):
    silu_gate = jax.nn.silu(gate_preact.astype(jnp.float32))
    hidden = (silu_gate * up_output.astype(jnp.float32)).astype(jnp.bfloat16)
    hidden_grad = lax.dot_general(output_grad, down_weight, (((1,), (1,)), ((), ())), preferred_element_type=jnp.float32)
    up_grad = (hidden_grad * silu_gate).astype(jnp.bfloat16)
    down_in = jnp.dot(hidden, hidden_basis, preferred_element_type=jnp.float32)
    up_out = jnp.dot(up_grad, up_basis, preferred_element_type=jnp.float32)
    down_out = jnp.dot(output_grad, output_basis, preferred_element_type=jnp.float32)
    up_in = jnp.dot(normed_input, normed_basis, preferred_element_type=jnp.float32)
    member = jax.vmap(partial(segment_matrix, TOK))(lengths)

    def grouped(values):
        return values.reshape(GROUPS, TOK, R)
    down_sum = jnp.einsum('gte,gti,gtj->geij', member, grouped(down_out), grouped(down_in), precision=lax.Precision.HIGHEST)
    up_sum = jnp.einsum('gte,gti,gtj->geij', member, grouped(up_out), grouped(up_in), precision=lax.Precision.HIGHEST)
    stacked = jnp.concatenate([down_sum.reshape(EXAMPLES, R * R), up_sum.reshape(EXAMPLES, R * R)], axis=1)
    unit_rows = (stacked * lax.rsqrt(lax.optimization_barrier(jnp.mean(stacked * stacked, axis=1, keepdims=True)) + 1e-06)).astype(jnp.bfloat16)
    raw_scores = lax.dot_general(unit_rows, val_bank, (((1,), (1,)), ((), ())), preferred_element_type=jnp.float32)
    return raw_scores * (2 * R * R) ** (-0.5)
```

```python
import functools

import jax
import jax.numpy as jnp
from jax import lax
from jax.experimental import pallas as pl
from jax.experimental.pallas import tpu as pltpu
from jax.sharding import PartitionSpec as P

R = 64
EPS = 1e-06
AXES = ("dp", "tensor")
NT = (((1,), (1,)), ((), ()))
VMEM_BYTES = 48 * 1024 * 1024


def after(value, *others):
    return lax.optimization_barrier((value,) + others)[0]


def silu(gate):
    return gate / (1.0 + jnp.exp(-gate))


def pack(rows):
    half = rows.shape[0] // 2
    return jnp.concatenate([rows[:half], rows[half:]], axis=1)


def unpack(rows):
    return jnp.concatenate([rows[:, :R], rows[:, R:]], axis=0)


def project_kernel(pieces, parts, per_piece, *refs):
    gates = refs[:pieces]
    grads = refs[pieces : pieces + parts]
    weights = refs[pieces + parts : pieces + 2 * parts]
    basis, before, out, act, total = refs[pieces + 2 * parts :]
    step = pl.program_id(0)

    @pl.when(step == 0)
    def _():
        total[...] = jnp.zeros_like(total)

    for index, gate in enumerate(gates):

        @pl.when(step // per_piece == index)
        def _(gate=gate):
            act[...] = silu(gate[...].astype(jnp.float32))

    hidden_grad = sum(
        lax.dot_general(grad[...], weight[...], NT, preferred_element_type=jnp.float32)
        for grad, weight in zip(grads, weights, strict=True)
    )
    up_grad = (hidden_grad * act[...]).astype(jnp.bfloat16)
    total[...] += jnp.dot(up_grad, basis[...], preferred_element_type=jnp.float32)

    @pl.when(step == pl.num_programs(0) - 1)
    def _():
        out[...] = before[...] + pack(total[...])


def project(gates, grads, weights, basis, before, start, width, tile):
    pieces, parts = len(gates), len(grads)
    rows, depth = grads[0].shape
    per_piece = width // pieces // tile
    steps = width // tile
    first = start // tile

    def gate_spec(index, column):
        return pl.BlockSpec(
            (rows, tile),
            lambda i: (0, column // tile + jnp.clip(i - index * per_piece, 0, per_piece - 1)),
        )

    whole = lambda i: (0, 0)
    return pl.pallas_call(
        functools.partial(project_kernel, pieces, parts, per_piece),
        grid=(steps,),
        in_specs=[gate_spec(index, column) for index, (_, column) in enumerate(gates)]
        + [pl.BlockSpec((rows, depth), whole)] * parts
        + [pl.BlockSpec((tile, depth), lambda i, block=block: (first + i, block)) for _, block in weights]
        + [pl.BlockSpec((tile, R), lambda i: (first + i, 0)), pl.BlockSpec((rows // 2, 2 * R), whole)],
        out_specs=pl.BlockSpec((rows // 2, 2 * R), whole),
        out_shape=jax.ShapeDtypeStruct((rows // 2, 2 * R), jnp.float32),
        scratch_shapes=[pltpu.VMEM((rows, tile), jnp.float32), pltpu.VMEM((rows, R), jnp.float32)],
        compiler_params=pltpu.CompilerParams(vmem_limit_bytes=VMEM_BYTES),
        cost_estimate=pl.CostEstimate(
            flops=2 * rows * width * (parts * depth + R),
            bytes_accessed=2 * width * (parts * depth + rows) + 2 * rows * parts * depth,
            transcendentals=rows * width,
        ),
    )(*[g for g, _ in gates], *grads, *[w for w, _ in weights], basis, before)


def hidden_kernel(gate, up, basis, out):
    @pl.when(pl.program_id(0) == 0)
    def _():
        out[...] = jnp.zeros_like(out)

    hidden = (silu(gate[...].astype(jnp.float32)) * up[...].astype(jnp.float32)).astype(jnp.bfloat16)
    out[...] += jnp.dot(hidden, basis[...], preferred_element_type=jnp.float32)


def hidden_project(gate, up, basis, tile):
    rows, width = gate.shape
    return pl.pallas_call(
        hidden_kernel,
        grid=(width // tile,),
        in_specs=[
            pl.BlockSpec((rows, tile), lambda i: (0, i)),
            pl.BlockSpec((rows, tile), lambda i: (0, i)),
            pl.BlockSpec((tile, R), lambda i: (i, 0)),
        ],
        out_specs=pl.BlockSpec((rows, R), lambda i: (0, 0)),
        out_shape=jax.ShapeDtypeStruct((rows, R), jnp.float32),
        compiler_params=pltpu.CompilerParams(vmem_limit_bytes=VMEM_BYTES),
        cost_estimate=pl.CostEstimate(
            flops=2 * rows * width * R, bytes_accessed=4 * rows * width, transcendentals=rows * width
        ),
    )(gate, up, basis)


def score_kernel(examples, partials, masked, down_sum, down_val, up_val, out):
    up_out = unpack(sum(partials[n].astype(jnp.float32) for n in range(partials.shape[0])))
    up_sum = lax.dot_general(
        up_out.T,
        masked[...],
        (((1,), (0,)), ((), ())),
        precision=lax.Precision.HIGHEST,
        preferred_element_type=jnp.float32,
    )
    down = down_sum[...]
    squares = jnp.sum(up_sum * up_sum + down * down, axis=0, keepdims=True)
    lane = lax.broadcasted_iota(jnp.int32, (1, examples * R), 1) // R
    inverse = jnp.zeros_like(squares)
    for e in range(examples):
        mean = jnp.sum(jnp.where(lane == e, squares, 0.0), axis=1, keepdims=True) / (2 * R * R)
        inverse = jnp.where(lane == e, lax.rsqrt(mean + EPS), inverse)
    down = (down * inverse).astype(jnp.bfloat16).astype(jnp.float32)
    up_sum = (up_sum * inverse).astype(jnp.bfloat16).astype(jnp.float32)
    values = down_val.shape[0]
    columns = lax.broadcasted_iota(jnp.int32, (examples, values), 1)
    rows = lax.broadcasted_iota(jnp.int32, (examples, values), 0)
    scores = jnp.zeros((examples, values), jnp.float32)
    for v in range(values):
        both = down * down_val[v].astype(jnp.float32) + up_sum * up_val[v].astype(jnp.float32)
        by_lane = jnp.sum(both, axis=0, keepdims=True)
        for e in range(examples):
            one = jnp.sum(jnp.where(lane == e, by_lane, 0.0), axis=1, keepdims=True)
            scores = jnp.where((columns == v) & (rows == e), one, scores)
    out[...] = scores * float(2 * R * R) ** (-0.5)


def split(total, most, unit):
    for count in range(most, 0, -1):
        if total % (count * unit) == 0:
            return count
    return 1


def gather_line(grad, side, lane, place):
    depth = grad.shape[1] // 2
    ga, gb = grad[:, :depth], grad[:, depth:]
    spot = jnp.where(side == 0, place, 3 - place)

    def at(a, c, s):
        return (2 * a + c) * 4 + (s if a == 0 else 3 - s)

    def move(value, hops, other=False):
        pairs = [
            (at(1 - a if other else a, c, s), at(a, c, t)) for a in (0, 1) for c in (0, 1) for s, t in hops
        ]
        return lax.ppermute(value, AXES, pairs)

    def pick(*cases):
        value = cases[3]
        for s in (2, 1, 0):
            if cases[s] is not value:
                value = jnp.where(spot == s, cases[s], value)
        return value

    xa = move(ga, [(3, 0), (2, 1)], other=True)
    xb = move(gb, [(3, 2), (2, 3)], other=True)
    u1 = move(ga, [(0, 1), (1, 2)])
    v1 = move(ga, [(1, 0)])
    u2 = move(jnp.where(spot == 2, u1, xa), [(0, 1), (1, 2), (2, 3)])
    v2 = move(xa, [(1, 0)])
    u3 = move(jnp.where(spot == 1, u1, u2), [(1, 2), (2, 3)])
    v3 = move(after(gb, v2), [(1, 0)])
    u4 = move(jnp.where(spot == 1, u2, u3), [(1, 2), (2, 3)])
    v4 = move(after(xb, v2), [(2, 1), (3, 2)])
    u5 = move(jnp.where(spot == 2, u4, gb), [(0, 1), (1, 2), (2, 3)])
    v5 = move(after(v4, v3), [(1, 0), (2, 1)])
    u6 = move(u5, [(1, 2), (2, 3)])
    v6 = move(v5, [(1, 0)])
    u7 = move(after(xb, u6), [(2, 3)])
    u8 = move(after(u6, u7), [(2, 3)])

    swap = (side + lane) % 2 == 1

    def both(first, second):
        return (
            pick(*[jnp.where(swap, s, f) if s is not f else f for f, s in zip(first, second, strict=True)]),
            pick(*[jnp.where(swap, f, s) if s is not f else f for f, s in zip(first, second, strict=True)]),
        )

    return {
        "near_a": both((ga, u1, u3, u4), (v1, ga, u1, u2)),
        "far_a": both((xa, u2, u4, u5), (v2, xa, u2, u3)),
        "far_b": both((v5, v4, xb, u7), (v6, v5, v4, xb)),
        "near_b": both((gb, u5, u6, u8), (v3, gb, u5, u6)),
    }, xa


def gather_any(grad, side, lane):
    count = lax.axis_size("dp")
    whole = lax.all_gather(grad, "tensor", axis=1, tiled=True)
    block = whole.shape[1] // count
    far = lax.ppermute(
        lax.dynamic_slice_in_dim(whole, (1 - side) * 2 * block, 2 * block, axis=1),
        "dp",
        [(i, i ^ 2) for i in range(count)],
    )
    near = lax.dynamic_slice_in_dim(whole, side * 2 * block, 2 * block, axis=1)
    blocks = {}
    for name, value in (("near", near), ("far", far)):
        own = jnp.where(lane == 0, value[:, :block], value[:, block:])
        sibling = jnp.where(lane == 0, value[:, block:], value[:, :block])
        for half, cut in (("a", slice(0, block // 2)), ("b", slice(block // 2, block))):
            blocks[f"{name}_{half}"] = (own[:, cut], sibling[:, cut])
    return blocks, far


def sum_tensor(value):
    count = lax.axis_size("tensor")
    if count > 8:
        return lax.psum(value.astype(jnp.float32), "tensor")[None]
    return jnp.stack(
        [value]
        + [lax.ppermute(value, "tensor", [(i, (i + k) % count) for i in range(count)]) for k in range(1, count)]
    )


def body(
    gate_preact,
    up_output,
    normed_input,
    output_grad,
    down_weight,
    normed_basis,
    output_basis,
    hidden_basis,
    up_basis,
    val_bank,
    lengths,
):
    rows, width = gate_preact.shape
    examples = lengths.shape[1]
    index, place = lax.axis_index("dp"), lax.axis_index("tensor")
    side, lane = index // 2, index % 2
    count = lax.axis_size("dp")
    across = [(i, i ^ 2) for i in range(count)]
    beside = [(i, i ^ 1) for i in range(count)]

    if count == 4 and lax.axis_size("tensor") == 4:
        grads, first = gather_line(output_grad, side, lane, place)
    else:
        grads, first = gather_any(output_grad, side, lane)
    sibling = lax.ppermute(down_weight, "dp", beside)

    pieces = split(width, 7, 256)
    piece = width // pieces
    tile = piece // split(piece, max(1, piece // 512), 128)
    far_gates = []
    for n in range(pieces):
        own = after(gate_preact[:, n * piece : (n + 1) * piece], far_gates[n - 2] if n >= 2 else first)
        far_gates.append(lax.ppermute(own, "dp", across))

    totals = lax.psum(
        jnp.concatenate(
            [
                jnp.dot(output_grad, output_basis, preferred_element_type=jnp.float32),
                jnp.dot(normed_input, normed_basis, preferred_element_type=jnp.float32),
                hidden_project(gate_preact, up_output, hidden_basis, tile),
            ],
            axis=1,
        ),
        "tensor",
    )
    down_out, up_in, down_in = totals[:, :R], totals[:, R : 2 * R], totals[:, 2 * R :]
    ends = jnp.cumsum(lengths[0])
    owner = jnp.arange(examples * R, dtype=jnp.int32) // R
    token = jnp.arange(rows, dtype=jnp.int32)
    member = (token[:, None] >= (ends - lengths[0])[owner][None, :]) & (token[:, None] < ends[owner][None, :])
    masked_up = jnp.where(member, jnp.tile(up_in, (1, examples)), 0.0)
    down_sum = lax.dot_general(
        down_out,
        jnp.where(member, jnp.tile(down_in, (1, examples)), 0.0),
        (((0,), (0,)), ((), ())),
        precision=lax.Precision.HIGHEST,
        preferred_element_type=jnp.float32,
    )
    values = lax.all_gather(val_bank, "dp", axis=1, tiled=True)
    values = jnp.tile(values.reshape(values.shape[0], 2, R, R), (1, 1, 1, examples))

    def weights(*halves):
        return [(w, half) for half in halves for w in (down_weight, sibling)]

    zero = jnp.zeros((rows // 2, 2 * R), jnp.float32)
    near, far = zero, zero
    early = pieces - 1
    half = (pieces + 1) // 2

    def far_part(far, parts, begin, end):
        return project(
            [(far_gates[n], 0) for n in range(begin, end)],
            sum((grads["far_" + p] for p in parts), ()),
            weights(*[0 if p == "a" else 1 for p in parts]),
            up_basis,
            far,
            begin * piece,
            (end - begin) * piece,
            tile,
        )

    near = project([(gate_preact, 0)], grads["near_a"], weights(0), up_basis, near, 0, width, tile)
    if early > 0:
        far = far_part(far, "a", 0, half)
        if early > half:
            far = far_part(far, "a", half, early)
        far = far_part(far, "b", 0, early)
    far = far_part(far, "ab", early, pieces)
    back = lax.ppermute(far, "dp", across)
    near = project([(gate_preact, 0)], grads["near_b"], weights(1), up_basis, near, 0, width, tile)
    partials = sum_tensor((near + back).astype(jnp.bfloat16))
    return pl.pallas_call(
        functools.partial(score_kernel, examples),
        out_shape=jax.ShapeDtypeStruct((examples, val_bank.shape[0]), jnp.float32),
    )(partials, masked_up, down_sum, values[:, 0], values[:, 1])


def solution(mesh):
    placed = (
        P(("parts", "dp"), "tensor"),
        P(("parts", "dp"), "tensor"),
        P(("parts", "dp"), "tensor"),
        P(("parts", "dp"), "tensor"),
        P("tensor", "dp"),
        P("tensor", None),
        P("tensor", None),
        P("tensor", None),
        P("tensor", None),
        P("tensor", "dp"),
        P(("parts", "dp"), None),
    )
    return jax.shard_map(
        body, mesh=mesh, in_specs=placed, out_specs=P(("parts", "dp"), "tensor"), check_vma=False
    )
```

```python
import functools

import jax
import jax.numpy as jnp
from jax import lax
from jax.experimental import pallas as pl
from jax.experimental.pallas import tpu as pltpu
from jax.sharding import PartitionSpec as P

R = 64
EPS = 1e-06
AXES = ("dp", "tensor")
NT = (((1,), (1,)), ((), ()))
VMEM_BYTES = 48 * 1024 * 1024


def after(value, *others):
    return lax.optimization_barrier((value,) + others)[0]


def silu(gate):
    return gate / (1.0 + jnp.exp(-gate))


def pack(rows):
    half = rows.shape[0] // 2
    return jnp.concatenate([rows[:half], rows[half:]], axis=1)


def unpack(rows):
    return jnp.concatenate([rows[:, :R], rows[:, R:]], axis=0)


def project_kernel(pieces, parts, per_piece, _, *refs):
    gates = refs[:pieces]
    grads = refs[pieces : pieces + parts]
    weights = refs[pieces + parts : pieces + 2 * parts]
    basis, before, out, act, total = refs[pieces + 2 * parts :]
    step = pl.program_id(0)

    @pl.when(step == 0)
    def _():
        total[...] = jnp.zeros_like(total)

    for index, gate in enumerate(gates):

        @pl.when(step // per_piece == index)
        def _(gate=gate):
            act[...] = silu(gate[...].astype(jnp.float32))

    hidden_grad = sum(
        lax.dot_general(grad[...], weight[...], NT, preferred_element_type=jnp.float32)
        for grad, weight in zip(grads, weights, strict=True)
    )
    up_grad = (hidden_grad * act[...]).astype(jnp.bfloat16)
    total[...] += jnp.dot(up_grad, basis[...], preferred_element_type=jnp.float32)

    @pl.when(step == pl.num_programs(0) - 1)
    def _():
        out[...] = before[...] + pack(total[...])


def project(gates, grads, weights, half, basis, before, start, width, tile):
    pieces = len(gates)
    pairs = [(g, block, w) for w, group in zip(weights, grads, strict=True) for g, block in group]
    parts = len(pairs)
    rows, depth = pairs[0][0].shape
    own = gates[0].shape[1] * pieces == width
    per_piece = width // pieces // tile
    first = start // tile
    whole = lambda i, _: (0, 0)

    def gate_spec(index):
        if own:
            return pl.BlockSpec((rows, tile), lambda i, _: (0, jnp.clip(i - index * per_piece, 0, per_piece - 1)))
        return pl.BlockSpec((rows, tile), lambda i, _: (0, first + i))

    def weight_spec(block):
        if block is None:
            return pl.BlockSpec((tile, depth), lambda i, half: (first + i, half[0]))
        if block == "other":
            return pl.BlockSpec((tile, depth), lambda i, half: (first + i, 1 - half[0]))
        return pl.BlockSpec((tile, depth), lambda i, _: (first + i, block))

    return pl.pallas_call(
        functools.partial(project_kernel, pieces, parts, per_piece),
        grid_spec=pltpu.PrefetchScalarGridSpec(
            num_scalar_prefetch=1,
            grid=(width // tile,),
            in_specs=[gate_spec(index) for index in range(pieces)]
            + [pl.BlockSpec((rows, depth), whole)] * parts
            + [weight_spec(block) for _, block, _ in pairs]
            + [pl.BlockSpec((tile, R), lambda i, _: (first + i, 0)), pl.BlockSpec((rows // 2, 2 * R), whole)],
            out_specs=pl.BlockSpec((rows // 2, 2 * R), whole),
            scratch_shapes=[pltpu.VMEM((rows, tile), jnp.float32), pltpu.VMEM((rows, R), jnp.float32)],
        ),
        out_shape=jax.ShapeDtypeStruct((rows // 2, 2 * R), jnp.float32),
        compiler_params=pltpu.CompilerParams(vmem_limit_bytes=VMEM_BYTES),
        cost_estimate=pl.CostEstimate(flops=0, bytes_accessed=0, transcendentals=0),
    )(half, *gates, *[g for g, _, _ in pairs], *[w for _, _, w in pairs], basis, before)


def local_kernel(gate, up, grad, normed, hidden_basis, output_basis, normed_basis, out):
    half = grad.shape[0] // 2

    @pl.when(pl.program_id(0) == 0)
    def _():
        out[:half] = pack(jnp.dot(grad[...], output_basis[...], preferred_element_type=jnp.float32))
        out[half : 2 * half] = pack(jnp.dot(normed[...], normed_basis[...], preferred_element_type=jnp.float32))
        out[2 * half :] = jnp.zeros((half, 2 * R), jnp.float32)

    hidden = (silu(gate[...].astype(jnp.float32)) * up[...].astype(jnp.float32)).astype(jnp.bfloat16)
    out[2 * half :] += pack(jnp.dot(hidden, hidden_basis[...], preferred_element_type=jnp.float32))


def local_products(gate, up, grad, normed, hidden_basis, output_basis, normed_basis, tile):
    rows, width = gate.shape
    whole = lambda i: (0, 0)
    return pl.pallas_call(
        local_kernel,
        grid=(width // tile,),
        in_specs=[
            pl.BlockSpec((rows, tile), lambda i: (0, i)),
            pl.BlockSpec((rows, tile), lambda i: (0, i)),
            pl.BlockSpec(grad.shape, whole),
            pl.BlockSpec(normed.shape, whole),
            pl.BlockSpec((tile, R), lambda i: (i, 0)),
            pl.BlockSpec(output_basis.shape, whole),
            pl.BlockSpec(normed_basis.shape, whole),
        ],
        out_specs=pl.BlockSpec((rows * 3 // 2, 2 * R), whole),
        out_shape=jax.ShapeDtypeStruct((rows * 3 // 2, 2 * R), jnp.float32),
        compiler_params=pltpu.CompilerParams(vmem_limit_bytes=VMEM_BYTES),
        cost_estimate=pl.CostEstimate(flops=0, bytes_accessed=0, transcendentals=0),
    )(gate, up, grad, normed, hidden_basis, output_basis, normed_basis)


def member_kernel(examples, lengths, *refs):
    parts, masked_up, down_sum = refs[:-2], refs[-2], refs[-1]
    totals = sum(part[n].astype(jnp.float32) for part in parts for n in range(part.shape[0]))
    half = totals.shape[0] // 3
    down_out, up_in, down_in = (unpack(totals[n * half : (n + 1) * half]) for n in range(3))
    token = lax.broadcasted_iota(jnp.int32, (2 * half, R), 0)
    begin = 0
    up, down = [], []
    for e in range(examples):
        end = begin + lengths[0, e]
        inside = (token >= begin) & (token < end)
        up.append(jnp.where(inside, up_in, 0.0))
        down.append(jnp.where(inside, down_in, 0.0))
        begin = end
    masked_up[...] = jnp.concatenate(up, axis=1)
    down_sum[...] = lax.dot_general(
        down_out.T,
        jnp.concatenate(down, axis=1),
        (((1,), (0,)), ((), ())),
        precision=lax.Precision.HIGHEST,
        preferred_element_type=jnp.float32,
    )


def member_products(lengths, parts, rows):
    examples = lengths.shape[1]
    return pl.pallas_call(
        functools.partial(member_kernel, examples),
        in_specs=[pl.BlockSpec(memory_space=pltpu.SMEM)] + [pl.BlockSpec(memory_space=pltpu.VMEM)] * len(parts),
        out_shape=(
            jax.ShapeDtypeStruct((rows, examples * R), jnp.float32),
            jax.ShapeDtypeStruct((R, examples * R), jnp.float32),
        ),
        cost_estimate=pl.CostEstimate(flops=0, bytes_accessed=0, transcendentals=0),
    )(lengths, *parts)


def score_kernel(examples, masked, down_sum, bank, *refs):
    partials, out = refs[:-1], refs[-1]
    up_out = unpack(sum(part[n].astype(jnp.float32) for part in partials for n in range(part.shape[0])))
    up_sum = lax.dot_general(
        up_out.T,
        masked[...],
        (((1,), (0,)), ((), ())),
        precision=lax.Precision.HIGHEST,
        preferred_element_type=jnp.float32,
    )
    down = down_sum[...]
    squares = jnp.sum(up_sum * up_sum + down * down, axis=0, keepdims=True)
    lane = lax.broadcasted_iota(jnp.int32, (1, examples * R), 1) // R
    inverse = jnp.zeros_like(squares)
    for e in range(examples):
        mean = jnp.sum(jnp.where(lane == e, squares, 0.0), axis=1, keepdims=True) / (2 * R * R)
        inverse = jnp.where(lane == e, lax.rsqrt(mean + EPS), inverse)
    down = (down * inverse).astype(jnp.bfloat16).astype(jnp.float32)
    up_sum = (up_sum * inverse).astype(jnp.bfloat16).astype(jnp.float32)
    values = bank.shape[0]
    columns = lax.broadcasted_iota(jnp.int32, (examples, values), 1)
    rows = lax.broadcasted_iota(jnp.int32, (examples, values), 0)
    scores = jnp.zeros((examples, values), jnp.float32)
    for v in range(values):
        row = jnp.concatenate([bank[v].astype(jnp.float32)] * examples, axis=1)
        both = down * row[:R] + up_sum * row[R:]
        by_lane = jnp.sum(both, axis=0, keepdims=True)
        for e in range(examples):
            one = jnp.sum(jnp.where(lane == e, by_lane, 0.0), axis=1, keepdims=True)
            scores = jnp.where((columns == v) & (rows == e), one, scores)
    out[...] = scores * float(2 * R * R) ** (-0.5)


def split(total, most, unit):
    for count in range(most, 0, -1):
        if total % (count * unit) == 0:
            return count
    return 1


class Line:
    def __init__(self, side, lane, place):
        self.spot = jnp.where(side == 0, place, 3 - place)
        self.even = (side + lane) % 2

    @staticmethod
    def at(a, c, s):
        return (2 * a + c) * 4 + (s if a == 0 else 3 - s)

    def move(self, value, hops, other=False):
        pairs = [
            (self.at(1 - a if other else a, c, s), self.at(a, c, t)) for a in (0, 1) for c in (0, 1) for s, t in hops
        ]
        return lax.ppermute(value, AXES, pairs)

    def pair(self, value):
        return self.move(value, [(0, 1), (1, 0), (2, 3), (3, 2)])

    def middle(self, value):
        return self.move(value, [(1, 2), (2, 1)])

    def outward(self, value):
        return self.move(value, [(1, 0), (2, 3)])

    def by_block(self, first, second, parity):
        keep = parity == self.even
        return jnp.where(keep, first, second), jnp.where(keep, second, first)


def gather_any(grad, side, lane):
    count = lax.axis_size("dp")
    whole = lax.all_gather(grad, "tensor", axis=1, tiled=True)
    block = whole.shape[1] // count
    far = lax.ppermute(
        lax.dynamic_slice_in_dim(whole, (1 - side) * 2 * block, 2 * block, axis=1),
        "dp",
        [(i, i ^ 2) for i in range(count)],
    )
    near = lax.dynamic_slice_in_dim(whole, side * 2 * block, 2 * block, axis=1)
    return [
        (jnp.where(lane == 0, v[:, :block], v[:, block:]), jnp.where(lane == 0, v[:, block:], v[:, :block]))
        for v in (near, far)
    ]


def all_tensor(value):
    count = lax.axis_size("tensor")
    if count > 8:
        return [lax.psum(value.astype(jnp.float32), "tensor")[None]]
    return [value[None]] + [
        lax.ppermute(value, "tensor", [(i, (i + k) % count) for i in range(count)])[None] for k in range(1, count)
    ]


def body(
    gate_preact,
    up_output,
    normed_input,
    output_grad,
    down_weight,
    normed_basis,
    output_basis,
    hidden_basis,
    up_basis,
    val_bank,
    lengths,
):
    rows, width = gate_preact.shape
    examples = lengths.shape[1]
    index, place = lax.axis_index("dp"), lax.axis_index("tensor")
    side, lane = index // 2, index % 2
    count = lax.axis_size("dp")
    across = [(i, i ^ 2) for i in range(count)]
    beside = [(i, i ^ 1) for i in range(count)]

    def local(tile):
        return local_products(
            gate_preact, up_output, output_grad, normed_input, hidden_basis, output_basis, normed_basis, tile
        )

    def turned_bank(value):
        return [value] + [
            lax.ppermute(value, "dp", [((i + k) % count, i) for i in range(count)]) for k in range(1, count)
        ]

    def straight_bank(turned):
        turned = jnp.stack(turned + turned)
        blocks = lax.dynamic_slice_in_dim(turned, (count - index) % count, count, axis=0)
        return jnp.concatenate([blocks[n] for n in range(count)], axis=1).reshape(val_bank.shape[0], 2 * R, R)

    zero = jnp.zeros((rows // 2, 2 * R), jnp.float32)
    sibling = lax.ppermute(down_weight, "dp", beside)
    both = (down_weight, sibling)

    if count == 4 and lax.axis_size("tensor") == 4 and width % (7 * 128) == 0:
        line = Line(side, lane, place)
        depth = output_grad.shape[1] // 2
        ga, gb = output_grad[:, :depth], output_grad[:, depth:]
        half = (line.spot // 2).astype(jnp.int32)[None]
        inner = (line.spot == 1) | (line.spot == 2)
        piece = width // 7
        tile = piece

        def cut(source, begin, end):
            return source[:, begin * piece : end * piece]

        def project_far(far, sources, grads, start):
            width = sum(source.shape[1] for source in sources)
            return project(sources, grads, both, half, up_basis, far, start * piece, width, tile)

        def project_near(near, grads):
            return project([gate_preact], grads, both, half, up_basis, near, 0, width, tile)

        xb = line.move(gb, [(3, 2), (2, 3)], other=True)
        ns = line.move(gb, [(0, 2), (1, 3)])
        xa = line.move(ga, [(3, 0), (2, 1)], other=True)
        s0 = lax.ppermute(cut(gate_preact, 0, 2), "dp", across)
        sums = local(piece)

        xa, xb, ns, sums, rest = lax.optimization_barrier((xa, xb, ns, sums, gate_preact))
        own_f = jnp.where(line.spot < 2, xa, xb)
        own_n = jnp.where(line.spot < 2, ga, ns)
        e_f, m_f = line.pair(own_f), line.middle(own_f)
        s2 = lax.ppermute(cut(rest, 2, 3), "dp", across)

        e_f, m_f, own_n, s0, sibling, rest = lax.optimization_barrier((e_f, m_f, own_n, s0, sibling, rest))
        both = (down_weight, sibling)
        mm_f, o_f = line.middle(e_f), line.outward(m_f)
        e_n, m_n = line.pair(own_n), line.middle(own_n)
        s3 = lax.ppermute(cut(rest, 3, 5), "dp", across)
        first_f = [[(g, None)] for g in line.by_block(own_f, e_f, line.spot % 2)]
        far = project_far(zero, [s0], first_f, 0)
        far = project_far(far, [s2], first_f, 2)

        mm_f, o_f, e_n, m_n, rest, far = lax.optimization_barrier((mm_f, o_f, e_n, m_n, rest, far))
        oo_f = line.outward(mm_f)
        mm_n, o_n = line.middle(e_n), line.outward(m_n)
        s5 = lax.ppermute(cut(rest, 5, 7), "dp", across)
        first_n = [[(g, None)] for g in line.by_block(own_n, e_n, line.spot % 2)]
        near = project_near(zero, first_n)
        far = project_far(far, [s3], first_f, 3)

        oo_f, mm_n, o_n, near, far, bank = lax.optimization_barrier((oo_f, mm_n, o_n, near, far, val_bank))
        oo_n = line.outward(mm_n)
        turned = turned_bank(bank)
        rest_f = line.by_block(jnp.where(inner, m_f, o_f), jnp.where(inner, mm_f, oo_f), line.spot // 2)
        rest_f = [[(g, "other")] for g in rest_f]
        all_f = [a + b for a, b in zip(first_f, rest_f, strict=True)]
        far = project_far(far, [s0], rest_f, 0)
        far = project_far(far, [s2], rest_f, 2)
        far = project_far(far, [s3], rest_f, 3)
        far = project_far(far, [s5], all_f, 5)
        back = lax.ppermute(far, "dp", across)

        oo_n, far, sums, turned = lax.optimization_barrier((oo_n, far, sums, turned))
        sums = all_tensor(sums.astype(jnp.bfloat16))
        bank = straight_bank(turned)
        rest_n = line.by_block(jnp.where(inner, m_n, o_n), jnp.where(inner, mm_n, oo_n), line.spot // 2)
        near = project_near(after(near, far), [[(g, "other")] for g in rest_n])
        partials = all_tensor((near + back).astype(jnp.bfloat16))
        masked_up, down_sum = member_products(lengths, list(lax.optimization_barrier((*sums, near))[:-1]), rows)
    else:
        half = jnp.zeros((1,), jnp.int32)
        near_grads, far_grads = gather_any(output_grad, side, lane)
        far_gate = lax.ppermute(gate_preact, "dp", across)
        tile = width // split(width, max(1, width // 512), 128)
        masked_up, down_sum = member_products(lengths, all_tensor(local(tile)), rows)
        bank = straight_bank(turned_bank(val_bank))
        far = project([far_gate], [[(g, 0)] for g in far_grads], both, half, up_basis, zero, 0, width, tile)
        back = lax.ppermute(far, "dp", across)
        near = project([gate_preact], [[(g, 0)] for g in near_grads], both, half, up_basis, zero, 0, width, tile)
        partials = all_tensor((near + back).astype(jnp.bfloat16))

    return pl.pallas_call(
        functools.partial(score_kernel, examples),
        out_shape=jax.ShapeDtypeStruct((examples, val_bank.shape[0]), jnp.float32),
    )(masked_up, down_sum, bank, *partials)


def solution(mesh):
    placed = (
        P(("parts", "dp"), "tensor"),
        P(("parts", "dp"), "tensor"),
        P(("parts", "dp"), "tensor"),
        P(("parts", "dp"), "tensor"),
        P("tensor", "dp"),
        P("tensor", None),
        P("tensor", None),
        P("tensor", None),
        P("tensor", None),
        P("tensor", "dp"),
        P(("parts", "dp"), None),
    )
    return jax.shard_map(
        body, mesh=mesh, in_specs=placed, out_specs=P(("parts", "dp"), "tensor"), check_vma=False
    )
```

```python
import functools

import jax
import jax.numpy as jnp
from jax import lax
from jax.experimental import pallas as pl
from jax.experimental.pallas import tpu as pltpu
from jax.sharding import PartitionSpec as P

R = 64
EPS = 1e-06
AXES = ("dp", "tensor")
NT = (((1,), (1,)), ((), ()))
VMEM_BYTES = 48 * 1024 * 1024


def after(value, *others):
    return lax.optimization_barrier((value,) + others)[0]


def silu(gate):
    return 0.5 * gate * (1.0 + jnp.tanh(0.5 * gate))


def project_kernel(bounds, parts, _, *refs):
    pieces = len(bounds) - 1
    gates = refs[:pieces]
    grads = refs[pieces : pieces + parts]
    weights = refs[pieces + parts : pieces + 2 * parts]
    basis, before, out, act = refs[pieces + 2 * parts :]
    step = pl.program_id(0)

    @pl.when(step == 0)
    def _():
        out[...] = before[...]

    for index, gate in enumerate(gates):

        @pl.when((step >= bounds[index]) & (step < bounds[index + 1]))
        def _(gate=gate):
            act[...] = silu(gate[...].astype(jnp.float32))

    hidden_grad = sum(
        lax.dot_general(grad[...], weight[...], NT, preferred_element_type=jnp.float32)
        for grad, weight in zip(grads, weights, strict=True)
    )
    up_grad = (hidden_grad * act[...]).astype(jnp.bfloat16)
    out[...] += lax.dot_general(basis[...], up_grad, NT, preferred_element_type=jnp.float32)


def project(gates, grads, weights, half, basis, before, start, tile):
    gates = [gate if isinstance(gate, tuple) else (gate, 0, gate.shape[1]) for gate in gates]
    bounds = [0]
    for _, _, width in gates:
        bounds.append(bounds[-1] + width // tile)
    pairs = [(g, block, w) for w, group in zip(weights, grads, strict=True) for g, block in group]
    parts = len(pairs)
    rows, depth = pairs[0][0].shape
    first = start // tile
    whole = lambda i, _: (0, 0)

    def gate_spec(index):
        low, high, skip = bounds[index], bounds[index + 1], gates[index][1] // tile
        return pl.BlockSpec((rows, tile), lambda i, _: (0, skip + jnp.clip(i - low, 0, high - low - 1)))

    def weight_spec(block):
        if block is None:
            return pl.BlockSpec((tile, depth), lambda i, half: (first + i, half[0]))
        if block == "other":
            return pl.BlockSpec((tile, depth), lambda i, half: (first + i, 1 - half[0]))
        return pl.BlockSpec((tile, depth), lambda i, _: (first + i, block))

    return pl.pallas_call(
        functools.partial(project_kernel, bounds, parts),
        grid_spec=pltpu.PrefetchScalarGridSpec(
            num_scalar_prefetch=1,
            grid=(bounds[-1],),
            in_specs=[gate_spec(index) for index in range(len(gates))]
            + [pl.BlockSpec((rows, depth), whole)] * parts
            + [weight_spec(block) for _, block, _ in pairs]
            + [pl.BlockSpec((R, tile), lambda i, _: (0, first + i)), pl.BlockSpec((R, rows), whole)],
            out_specs=pl.BlockSpec((R, rows), whole),
            scratch_shapes=[pltpu.VMEM((rows, tile), jnp.float32)],
        ),
        out_shape=jax.ShapeDtypeStruct((R, rows), jnp.float32),
        compiler_params=pltpu.CompilerParams(vmem_limit_bytes=VMEM_BYTES),
        cost_estimate=pl.CostEstimate(flops=1, bytes_accessed=1, transcendentals=0),
    )(half, *[gate for gate, _, _ in gates], *[g for g, _, _ in pairs], *[w for _, _, w in pairs], basis, before)


def local_kernel(cuts, gate, up, grad, normed, hidden_basis, output_basis, normed_basis, out, *cut_gates):
    step = pl.program_id(0)

    @pl.when(step == 0)
    def _():
        out[:R] = lax.dot_general(output_basis[...], grad[...], NT, preferred_element_type=jnp.float32)
        out[R : 2 * R] = lax.dot_general(normed_basis[...], normed[...], NT, preferred_element_type=jnp.float32)
        out[2 * R :] = jnp.zeros((R, out.shape[1]), jnp.float32)

    value = gate[...].astype(jnp.float32)
    hidden = (silu(value) * up[...].astype(jnp.float32)).astype(jnp.bfloat16)
    out[2 * R :] += lax.dot_general(hidden_basis[...], hidden, NT, preferred_element_type=jnp.float32)
    for (low, high), piece in zip(cuts, cut_gates, strict=True):

        @pl.when((step >= low) & (step < high))
        def _(piece=piece):
            piece[...] = gate[...]


def local_products(gate, up, grad, normed, hidden_basis, output_basis, normed_basis, tile, cuts=()):
    rows, width = gate.shape
    whole = lambda i: (0, 0)

    def cut_spec(low, high):
        return pl.BlockSpec((rows, tile), lambda i: (0, jnp.clip(i - low, 0, high - low - 1)))

    return pl.pallas_call(
        functools.partial(local_kernel, cuts),
        grid=(width // tile,),
        in_specs=[
            pl.BlockSpec((rows, tile), lambda i: (0, i)),
            pl.BlockSpec((rows, tile), lambda i: (0, i)),
            pl.BlockSpec(grad.shape, whole),
            pl.BlockSpec(normed.shape, whole),
            pl.BlockSpec((R, tile), lambda i: (0, i)),
            pl.BlockSpec(output_basis.shape, whole),
            pl.BlockSpec(normed_basis.shape, whole),
        ],
        out_specs=[pl.BlockSpec((3 * R, rows), whole)] + [cut_spec(*cut) for cut in cuts],
        out_shape=[jax.ShapeDtypeStruct((3 * R, rows), jnp.float32)]
        + [jax.ShapeDtypeStruct((rows, (high - low) * tile), gate.dtype) for low, high in cuts],
        compiler_params=pltpu.CompilerParams(vmem_limit_bytes=VMEM_BYTES),
        cost_estimate=pl.CostEstimate(flops=1, bytes_accessed=1, transcendentals=0),
    )(gate, up, grad, normed, hidden_basis, output_basis, normed_basis)


def by_example(lengths, value):
    token = lax.broadcasted_iota(jnp.int32, value.shape, 1)
    begin, members = 0, []
    for e in range(lengths.shape[1]):
        end = begin + lengths[0, e]
        members.append(jnp.where((token >= begin) & (token < end), value, 0.0))
        begin = end
    return jnp.concatenate(members, axis=0)


def outer_sums(lengths, left, right):
    return lax.dot_general(
        by_example(lengths, left),
        right,
        NT,
        precision=lax.Precision.HIGHEST,
        preferred_element_type=jnp.float32,
    )


def down_kernel(lengths, *refs):
    parts, (blocks, up_in, down_sum, bank) = refs[:-4], refs[-4:]
    totals = sum(part[...] for part in parts)
    up_in[...] = totals[R : 2 * R]
    down_sum[...] = outer_sums(lengths, totals[:R], totals[2 * R :])
    count, _, block, _ = blocks.shape
    for n in range(count):
        bank[:, n * block : (n + 1) * block, :] = blocks[n].astype(jnp.float32)


def down_products(lengths, parts, blocks):
    examples = lengths.shape[1]
    count, values, block, _ = blocks.shape
    return pl.pallas_call(
        down_kernel,
        in_specs=[pl.BlockSpec(memory_space=pltpu.SMEM)] + [pl.BlockSpec(memory_space=pltpu.VMEM)] * (len(parts) + 1),
        out_shape=(
            jax.ShapeDtypeStruct((R, parts[0].shape[1]), jnp.float32),
            jax.ShapeDtypeStruct((examples * R, R), jnp.float32),
            jax.ShapeDtypeStruct((values, count * block, R), jnp.float32),
        ),
        compiler_params=pltpu.CompilerParams(vmem_limit_bytes=VMEM_BYTES),
        cost_estimate=pl.CostEstimate(flops=1, bytes_accessed=1, transcendentals=0),
    )(lengths, *parts, blocks)


def score_kernel(lengths, up_in, down_sum, bank, *refs):
    partials, out = refs[:-1], refs[-1]
    up_sum = outer_sums(lengths, sum(part[...].astype(jnp.float32) for part in partials), up_in[...])
    values, examples = out.shape
    rows = lax.broadcasted_iota(jnp.int32, out.shape, 0)
    columns = lax.broadcasted_iota(jnp.int32, out.shape, 1)
    scores = jnp.zeros(out.shape, jnp.float32)
    for e in range(examples):
        down, up = down_sum[e * R : (e + 1) * R], up_sum[e * R : (e + 1) * R]
        mean = jnp.sum(down * down + up * up, axis=(0, 1), keepdims=True) / (2 * R * R)
        inverse = lax.rsqrt(mean + EPS)
        down = (down * inverse).astype(jnp.bfloat16).astype(jnp.float32)
        up = (up * inverse).astype(jnp.bfloat16).astype(jnp.float32)
        for v in range(values):
            one = jnp.sum(down * bank[v, :R] + up * bank[v, R:], axis=(0, 1), keepdims=True)
            scores = jnp.where((rows == v) & (columns == e), one, scores)
    out[...] = scores * float(2 * R * R) ** (-0.5)


def split(total, most, unit):
    for count in range(most, 0, -1):
        if total % (count * unit) == 0:
            return count
    return 1


class Line:
    def __init__(self, side, lane, place):
        self.spot = jnp.where(side == 0, place, 3 - place)
        self.even = (side + lane) % 2

    @staticmethod
    def at(a, c, s):
        return (2 * a + c) * 4 + (s if a == 0 else 3 - s)

    def move(self, value, hops, other=False):
        pairs = [
            (self.at(1 - a if other else a, c, s), self.at(a, c, t)) for a in (0, 1) for c in (0, 1) for s, t in hops
        ]
        return lax.ppermute(value, AXES, pairs)

    def pair(self, value):
        return self.move(value, [(0, 1), (1, 0), (2, 3), (3, 2)])

    def middle(self, value):
        return self.move(value, [(1, 2), (2, 1)])

    def outward(self, value):
        return self.move(value, [(1, 0), (2, 3)])

    def by_block(self, first, second, parity):
        keep = parity == self.even
        return jnp.where(keep, first, second), jnp.where(keep, second, first)


def gather_any(grad, side, lane):
    count = lax.axis_size("dp")
    whole = lax.all_gather(grad, "tensor", axis=1, tiled=True)
    block = whole.shape[1] // count
    far = lax.ppermute(
        lax.dynamic_slice_in_dim(whole, (1 - side) * 2 * block, 2 * block, axis=1),
        "dp",
        [(i, i ^ 2) for i in range(count)],
    )
    near = lax.dynamic_slice_in_dim(whole, side * 2 * block, 2 * block, axis=1)
    return [
        (jnp.where(lane == 0, v[:, :block], v[:, block:]), jnp.where(lane == 0, v[:, block:], v[:, :block]))
        for v in (near, far)
    ]


def all_tensor(value):
    count = lax.axis_size("tensor")
    if count > 8:
        return [lax.psum(value.astype(jnp.float32), "tensor")]
    return [value] + [
        lax.ppermute(value, "tensor", [(i, (i + k) % count) for i in range(count)]) for k in range(1, count)
    ]


def body(
    gate_preact,
    up_output,
    normed_input,
    output_grad,
    down_weight,
    normed_basis,
    output_basis,
    hidden_basis,
    up_basis,
    val_bank,
    lengths,
):
    rows, width = gate_preact.shape
    index, place = lax.axis_index("dp"), lax.axis_index("tensor")
    side, lane = index // 2, index % 2
    count = lax.axis_size("dp")
    across = [(i, i ^ 2) for i in range(count)]
    beside = [(i, i ^ 1) for i in range(count)]

    def local(tile, cuts=()):
        return local_products(
            gate_preact, up_output, output_grad, normed_input, hidden_basis.T, output_basis.T, normed_basis.T, tile, cuts
        )

    values = val_bank.reshape(val_bank.shape[0], -1, R)
    basis = up_basis.T
    zero = jnp.zeros((R, rows), jnp.float32)
    sibling = lax.ppermute(down_weight, "dp", beside)
    both = (down_weight, sibling)

    if count == 4 and lax.axis_size("tensor") == 4 and width % (7 * 128) == 0:
        line = Line(side, lane, place)
        depth = output_grad.shape[1] // 2
        ga, gb = output_grad[:, :depth], output_grad[:, depth:]
        half = (line.spot // 2).astype(jnp.int32)[None]
        inner = (line.spot == 1) | (line.spot == 2)
        tile = width // 7

        def exchange(value, apart):
            return lax.ppermute(value, "tensor", [(i, i ^ apart) for i in range(4)])

        def project_far(far, sources, grads, start):
            return project(sources, grads, both, half, basis, far, start * tile, tile)

        def project_near(near, grads, start, end):
            gate = (gate_preact, start * tile, (end - start) * tile)
            return project([gate], grads, both, half, basis, near, start * tile, tile)

        blocks = lax.all_gather(values, "dp", axis=0)
        xb = line.move(gb, [(3, 2), (2, 3)], other=True)
        ns = line.move(gb, [(0, 2), (1, 3)])
        xa = line.move(ga, [(3, 0), (2, 1)], other=True)
        s0 = lax.ppermute(gate_preact[:, : 2 * tile], "dp", across)
        sums, t2, t3, t5 = local(tile, ((2, 3), (3, 5), (5, 7)))

        ns, xa, xb, sums, t2, t3, t5 = lax.optimization_barrier((ns, xa, xb, sums, t2, t3, t5))
        own = jnp.concatenate([jnp.where(line.spot < 2, ga, ns), jnp.where(line.spot < 2, xa, xb)], axis=0)
        e, m = line.pair(own), line.middle(own)
        s2 = lax.ppermute(t2, "dp", across)

        e, m, sibling, s0, s2, t3, blocks = lax.optimization_barrier((e, m, sibling, s0, s2, t3, blocks))
        both = (down_weight, sibling)
        mm, o = line.middle(e), line.outward(m)
        first_n = line.by_block(own[:rows], e[:rows], line.spot % 2)
        first_f = line.by_block(own[rows:], e[rows:], line.spot % 2)
        first_n, first_f = [[(g, None)] for g in first_n], [[(g, None)] for g in first_f]
        s3 = lax.ppermute(t3, "dp", across)
        near = project_near(zero, first_n, 0, 7)
        far = project_far(zero, [s0, s2], first_f, 0)

        mm, o, s3, near, far, sums, t5 = lax.optimization_barrier((mm, o, s3, near, far, sums, t5))
        oo_f = line.outward(mm[rows:])
        s5 = lax.ppermute(t5, "dp", across)
        paired = exchange(sums, 1)
        third = jnp.where(inner, m, o)
        far = project_far(far, [s3], first_f, 3)

        oo_f, far, third, rest = lax.optimization_barrier((oo_f, far, third, mm))
        oo_n = line.outward(rest[:rows])
        rest_f = line.by_block(third[rows:], jnp.where(inner, rest[rows:], oo_f), line.spot // 2)
        rest_f = [[(g, "other")] for g in rest_f]
        all_f = [a + b for a, b in zip(first_f, rest_f, strict=True)]
        far = project_far(far, [s0, s2, s3], rest_f, 0)
        far = project_far(far, [s5], all_f, 5)

        oo_n, far, paired, sums, near = lax.optimization_barrier((oo_n, far, paired, sums, near))
        back = lax.ppermute(far, "dp", across)
        sums = sums + paired
        other = exchange(sums, 2)
        rest_n = line.by_block(third[:rows], jnp.where(inner, rest[:rows], oo_n), line.spot // 2)
        near = project_near(near, [[(g, "other")] for g in rest_n], 0, 7)

        near, back = lax.optimization_barrier((near, back))
        partials = all_tensor((near + back).astype(jnp.bfloat16))
        up_in, down_sum, bank = down_products(lengths, [sums, other], blocks)
    else:
        half = jnp.zeros((1,), jnp.int32)
        near_grads, far_grads = gather_any(output_grad, side, lane)
        far_gate = lax.ppermute(gate_preact, "dp", across)
        tile = width // split(width, max(1, width // 512), 128)
        up_in, down_sum, bank = down_products(
            lengths, all_tensor(local(tile)[0]), lax.all_gather(values, "dp", axis=0)
        )
        far = project([far_gate], [[(g, 0)] for g in far_grads], both, half, basis, zero, 0, tile)
        back = lax.ppermute(far, "dp", across)
        near = project([gate_preact], [[(g, 0)] for g in near_grads], both, half, basis, zero, 0, tile)
        partials = all_tensor((near + back).astype(jnp.bfloat16))

    return pl.pallas_call(
        score_kernel,
        in_specs=[pl.BlockSpec(memory_space=pltpu.SMEM)]
        + [pl.BlockSpec(memory_space=pltpu.VMEM)] * (3 + len(partials)),
        out_shape=jax.ShapeDtypeStruct((val_bank.shape[0], lengths.shape[1]), jnp.float32),
        compiler_params=pltpu.CompilerParams(vmem_limit_bytes=VMEM_BYTES),
    )(lengths, up_in, down_sum, bank, *partials).T


def solution(mesh):
    placed = (
        P(("parts", "dp"), "tensor"),
        P(("parts", "dp"), "tensor"),
        P(("parts", "dp"), "tensor"),
        P(("parts", "dp"), "tensor"),
        P("tensor", "dp"),
        P("tensor", None),
        P("tensor", None),
        P("tensor", None),
        P("tensor", None),
        P("tensor", "dp"),
        P(("parts", "dp"), None),
    )
    return jax.shard_map(
        body, mesh=mesh, in_specs=placed, out_specs=P(("parts", "dp"), "tensor"), check_vma=False
    )
```

```python
import functools

import jax
import jax.numpy as jnp
from jax import lax
from jax.experimental import pallas as pl
from jax.experimental.pallas import tpu as pltpu
from jax.sharding import PartitionSpec as P

R = 64
EPS = 1e-06
AXES = ("dp", "tensor")
NT = (((1,), (1,)), ((), ()))
VMEM_BYTES = 50 * 1024 * 1024


def after(value, *others):
    return lax.optimization_barrier((value,) + others)[0]


def silu(gate):
    return 0.5 * gate * (1.0 + jnp.tanh(0.5 * gate))


def project_kernel(bounds, parts, _, *refs):
    pieces = len(bounds) - 1
    gates = refs[:pieces]
    grads = refs[pieces : pieces + parts]
    weights = refs[pieces + parts : pieces + 2 * parts]
    basis, before, out, act = refs[pieces + 2 * parts :]
    step = pl.program_id(0)

    @pl.when(step == 0)
    def _():
        out[...] = before[...]

    for index, gate in enumerate(gates):

        @pl.when((step >= bounds[index]) & (step < bounds[index + 1]))
        def _(gate=gate):
            act[...] = silu(gate[...].astype(jnp.float32))

    hidden_grad = sum(
        lax.dot_general(grad[...], weight[...], NT, preferred_element_type=jnp.float32)
        for grad, weight in zip(grads, weights, strict=True)
    )
    up_grad = (hidden_grad * act[...]).astype(jnp.bfloat16)
    out[...] += lax.dot_general(basis[...], up_grad, NT, preferred_element_type=jnp.float32)


def project(gates, grads, weights, half, basis, before, start, tile):
    gates = [gate if isinstance(gate, tuple) else (gate, 0, gate.shape[1]) for gate in gates]
    bounds = [0]
    for _, _, width in gates:
        bounds.append(bounds[-1] + width // tile)
    pairs = [(g, block, w) for w, group in zip(weights, grads, strict=True) for g, block in group]
    parts = len(pairs)
    rows, depth = pairs[0][0].shape
    first = start // tile
    whole = lambda i, _: (0, 0)

    def gate_spec(index):
        low, high, skip = bounds[index], bounds[index + 1], gates[index][1] // tile
        return pl.BlockSpec((rows, tile), lambda i, _: (0, skip + jnp.clip(i - low, 0, high - low - 1)))

    def weight_spec(block):
        if block is None:
            return pl.BlockSpec((tile, depth), lambda i, half: (first + i, half[0]))
        if block == "other":
            return pl.BlockSpec((tile, depth), lambda i, half: (first + i, 1 - half[0]))
        return pl.BlockSpec((tile, depth), lambda i, _: (first + i, block))

    return pl.pallas_call(
        functools.partial(project_kernel, bounds, parts),
        grid_spec=pltpu.PrefetchScalarGridSpec(
            num_scalar_prefetch=1,
            grid=(bounds[-1],),
            in_specs=[gate_spec(index) for index in range(len(gates))]
            + [pl.BlockSpec((rows, depth), whole)] * parts
            + [weight_spec(block) for _, block, _ in pairs]
            + [pl.BlockSpec((R, tile), lambda i, _: (0, first + i)), pl.BlockSpec((R, rows), whole)],
            out_specs=pl.BlockSpec((R, rows), whole),
            scratch_shapes=[pltpu.VMEM((rows, tile), jnp.float32)],
        ),
        out_shape=jax.ShapeDtypeStruct((R, rows), jnp.float32),
        compiler_params=pltpu.CompilerParams(vmem_limit_bytes=VMEM_BYTES),
        cost_estimate=pl.CostEstimate(flops=1, bytes_accessed=1, transcendentals=0),
    )(half, *[gate for gate, _, _ in gates], *[g for g, _, _ in pairs], *[w for _, _, w in pairs], basis, before)


def local_kernel(cuts, gate, up, grad, normed, hidden_basis, output_basis, normed_basis, out, *cut_gates):
    step = pl.program_id(0)

    @pl.when(step == 0)
    def _():
        out[:R] = lax.dot_general(output_basis[...], grad[...], NT, preferred_element_type=jnp.float32)
        out[R : 2 * R] = lax.dot_general(normed_basis[...], normed[...], NT, preferred_element_type=jnp.float32)
        out[2 * R :] = jnp.zeros((R, out.shape[1]), jnp.float32)

    value = gate[...].astype(jnp.float32)
    hidden = (silu(value) * up[...].astype(jnp.float32)).astype(jnp.bfloat16)
    out[2 * R :] += lax.dot_general(hidden_basis[...], hidden, NT, preferred_element_type=jnp.float32)
    for (low, high), piece in zip(cuts, cut_gates, strict=True):

        @pl.when((step >= low) & (step < high))
        def _(piece=piece):
            piece[...] = gate[...]


def local_products(gate, up, grad, normed, hidden_basis, output_basis, normed_basis, tile, cuts=()):
    rows, width = gate.shape
    whole = lambda i: (0, 0)

    def cut_spec(low, high):
        return pl.BlockSpec((rows, tile), lambda i: (0, jnp.clip(i - low, 0, high - low - 1)))

    return pl.pallas_call(
        functools.partial(local_kernel, cuts),
        grid=(width // tile,),
        in_specs=[
            pl.BlockSpec((rows, tile), lambda i: (0, i)),
            pl.BlockSpec((rows, tile), lambda i: (0, i)),
            pl.BlockSpec(grad.shape, whole),
            pl.BlockSpec(normed.shape, whole),
            pl.BlockSpec((R, tile), lambda i: (0, i)),
            pl.BlockSpec(output_basis.shape, whole),
            pl.BlockSpec(normed_basis.shape, whole),
        ],
        out_specs=[pl.BlockSpec((3 * R, rows), whole)] + [cut_spec(*cut) for cut in cuts],
        out_shape=[jax.ShapeDtypeStruct((3 * R, rows), jnp.float32)]
        + [jax.ShapeDtypeStruct((rows, (high - low) * tile), gate.dtype) for low, high in cuts],
        compiler_params=pltpu.CompilerParams(vmem_limit_bytes=VMEM_BYTES),
        cost_estimate=pl.CostEstimate(flops=1, bytes_accessed=1, transcendentals=0),
    )(gate, up, grad, normed, hidden_basis, output_basis, normed_basis)


def by_example(lengths, value):
    token = lax.broadcasted_iota(jnp.int32, value.shape, 1)
    begin, members = 0, []
    for e in range(lengths.shape[1]):
        end = begin + lengths[0, e]
        members.append(jnp.where((token >= begin) & (token < end), value, 0.0))
        begin = end
    return jnp.concatenate(members, axis=0)


def outer_sums(lengths, left, right):
    return lax.dot_general(
        by_example(lengths, left),
        right,
        NT,
        precision=lax.Precision.HIGHEST,
        preferred_element_type=jnp.float32,
    )


def down_kernel(lengths, *refs):
    parts, (blocks, up_in, down_sum, bank) = refs[:-4], refs[-4:]
    totals = sum(part[...] for part in parts)
    up_in[...] = totals[R : 2 * R]
    down_sum[...] = outer_sums(lengths, totals[:R], totals[2 * R :])
    count, _, block, _ = blocks.shape
    for n in range(count):
        bank[:, n * block : (n + 1) * block, :] = blocks[n].astype(jnp.float32)


def down_products(lengths, parts, blocks):
    examples = lengths.shape[1]
    count, values, block, _ = blocks.shape
    return pl.pallas_call(
        down_kernel,
        in_specs=[pl.BlockSpec(memory_space=pltpu.SMEM)] + [pl.BlockSpec(memory_space=pltpu.VMEM)] * (len(parts) + 1),
        out_shape=(
            jax.ShapeDtypeStruct((R, parts[0].shape[1]), jnp.float32),
            jax.ShapeDtypeStruct((examples * R, R), jnp.float32),
            jax.ShapeDtypeStruct((values, count * block, R), jnp.float32),
        ),
        compiler_params=pltpu.CompilerParams(vmem_limit_bytes=VMEM_BYTES),
        cost_estimate=pl.CostEstimate(flops=1, bytes_accessed=1, transcendentals=0),
    )(lengths, *parts, blocks)


def score_kernel(lengths, up_in, down_sum, bank, *refs):
    partials, out = refs[:-1], refs[-1]
    up_sum = outer_sums(lengths, sum(part[...].astype(jnp.float32) for part in partials), up_in[...])
    values, examples = out.shape
    columns = lax.broadcasted_iota(jnp.int32, out.shape, 1)
    scores = jnp.zeros(out.shape, jnp.float32)
    for e in range(examples):
        down, up = down_sum[e * R : (e + 1) * R], up_sum[e * R : (e + 1) * R]
        mean = jnp.sum(jnp.sum(down * down + up * up, axis=0, keepdims=True), axis=1, keepdims=True) / (2 * R * R)
        inverse = lax.rsqrt(mean + EPS)
        down = (down * inverse).astype(jnp.bfloat16).astype(jnp.float32)
        up = (up * inverse).astype(jnp.bfloat16).astype(jnp.float32)
        by_column = [
            jnp.sum(down * bank[v, :R] + up * bank[v, R:], axis=0, keepdims=True) for v in range(values)
        ]
        one = jnp.sum(jnp.concatenate(by_column, axis=0), axis=1, keepdims=True)
        scores = jnp.where(columns == e, one, scores)
    out[...] = scores * float(2 * R * R) ** (-0.5)


def split(total, most, unit):
    for count in range(most, 0, -1):
        if total % (count * unit) == 0:
            return count
    return 1


class Line:
    def __init__(self, side, lane, place):
        self.spot = jnp.where(side == 0, place, 3 - place)
        self.even = (side + lane) % 2

    @staticmethod
    def at(a, c, s):
        return (2 * a + c) * 4 + (s if a == 0 else 3 - s)

    def move(self, value, hops, other=False):
        pairs = [
            (self.at(1 - a if other else a, c, s), self.at(a, c, t)) for a in (0, 1) for c in (0, 1) for s, t in hops
        ]
        return lax.ppermute(value, AXES, pairs)

    def pair(self, value):
        return self.move(value, [(0, 1), (1, 0), (2, 3), (3, 2)])

    def middle(self, value):
        return self.move(value, [(1, 2), (2, 1)])

    def outward(self, value):
        return self.move(value, [(1, 0), (2, 3)])

    def by_block(self, first, second, parity):
        keep = parity == self.even
        return jnp.where(keep, first, second), jnp.where(keep, second, first)


def gather_any(grad, side, lane):
    count = lax.axis_size("dp")
    whole = lax.all_gather(grad, "tensor", axis=1, tiled=True)
    block = whole.shape[1] // count
    far = lax.ppermute(
        lax.dynamic_slice_in_dim(whole, (1 - side) * 2 * block, 2 * block, axis=1),
        "dp",
        [(i, i ^ 2) for i in range(count)],
    )
    near = lax.dynamic_slice_in_dim(whole, side * 2 * block, 2 * block, axis=1)
    return [
        (jnp.where(lane == 0, v[:, :block], v[:, block:]), jnp.where(lane == 0, v[:, block:], v[:, :block]))
        for v in (near, far)
    ]


def all_tensor(value):
    count = lax.axis_size("tensor")
    if count > 8:
        return [lax.psum(value.astype(jnp.float32), "tensor")]
    return [value] + [
        lax.ppermute(value, "tensor", [(i, (i + k) % count) for i in range(count)]) for k in range(1, count)
    ]


def body(
    gate_preact,
    up_output,
    normed_input,
    output_grad,
    down_weight,
    normed_basis,
    output_basis,
    hidden_basis,
    up_basis,
    val_bank,
    lengths,
):
    rows, width = gate_preact.shape
    index, place = lax.axis_index("dp"), lax.axis_index("tensor")
    side, lane = index // 2, index % 2
    count = lax.axis_size("dp")
    across = [(i, i ^ 2) for i in range(count)]
    beside = [(i, i ^ 1) for i in range(count)]

    def local(tile, cuts=()):
        return local_products(
            gate_preact, up_output, output_grad, normed_input, hidden_basis.T, output_basis.T, normed_basis.T, tile, cuts
        )

    values = val_bank.reshape(val_bank.shape[0], -1, R)
    basis = up_basis.T
    zero = jnp.zeros((R, rows), jnp.float32)
    sibling = lax.ppermute(down_weight, "dp", beside)
    both = (down_weight, sibling)

    if count == 4 and lax.axis_size("tensor") == 4 and width % (7 * 128) == 0:
        line = Line(side, lane, place)
        depth = output_grad.shape[1] // 2
        ga, gb = output_grad[:, :depth], output_grad[:, depth:]
        half = (line.spot // 2).astype(jnp.int32)[None]
        inner = (line.spot == 1) | (line.spot == 2)
        tile = width // 7

        def exchange(value, apart):
            return lax.ppermute(value, "tensor", [(i, i ^ apart) for i in range(4)])

        def project_far(far, sources, grads, start):
            return project(sources, grads, both, half, basis, far, start * tile, tile)

        def project_near(near, grads, start, end):
            gate = (gate_preact, start * tile, (end - start) * tile)
            return project([gate], grads, both, half, basis, near, start * tile, tile)

        blocks = lax.all_gather(values, "dp", axis=0)
        xb = line.move(gb, [(3, 2), (2, 3)], other=True)
        ns = line.move(gb, [(0, 2), (1, 3)])
        xa = line.move(ga, [(3, 0), (2, 1)], other=True)
        s0 = lax.ppermute(gate_preact[:, : 2 * tile], "dp", across)
        sums, t2, t3, t5 = local(tile, ((2, 3), (3, 5), (5, 7)))

        ns, xa, xb, sums, t2, t3, t5 = lax.optimization_barrier((ns, xa, xb, sums, t2, t3, t5))
        own = jnp.concatenate([jnp.where(line.spot < 2, ga, ns), jnp.where(line.spot < 2, xa, xb)], axis=0)
        e, m = line.pair(own), line.middle(own)
        s2 = lax.ppermute(t2, "dp", across)

        e, m, sibling, s0, s2, t3, blocks = lax.optimization_barrier((e, m, sibling, s0, s2, t3, blocks))
        both = (down_weight, sibling)
        mm, o = line.middle(e), line.outward(m)
        first_n = line.by_block(own[:rows], e[:rows], line.spot % 2)
        first_f = line.by_block(own[rows:], e[rows:], line.spot % 2)
        first_n, first_f = [[(g, None)] for g in first_n], [[(g, None)] for g in first_f]
        s3 = lax.ppermute(t3, "dp", across)
        near = project_near(zero, first_n, 0, 7)
        far = project_far(zero, [s0, s2], first_f, 0)

        mm, o, s3, near, far, sums, t5 = lax.optimization_barrier((mm, o, s3, near, far, sums, t5))
        oo_f = line.outward(mm[rows:])
        s5 = lax.ppermute(t5, "dp", across)
        paired = exchange(sums, 1)
        third = jnp.where(inner, m, o)
        far = project_far(far, [s3], first_f, 3)

        oo_f, far, third, rest = lax.optimization_barrier((oo_f, far, third, mm))
        oo_n = line.outward(rest[:rows])
        rest_f = line.by_block(third[rows:], jnp.where(inner, rest[rows:], oo_f), line.spot // 2)
        rest_f = [[(g, "other")] for g in rest_f]
        all_f = [a + b for a, b in zip(first_f, rest_f, strict=True)]
        far = project_far(far, [s0, s2, s3], rest_f, 0)
        far = project_far(far, [s5], all_f, 5)

        oo_n, far, paired, sums, near = lax.optimization_barrier((oo_n, far, paired, sums, near))
        back = lax.ppermute(far, "dp", across)
        sums = sums + paired
        other = exchange(sums, 2)
        rest_n = line.by_block(third[:rows], jnp.where(inner, rest[:rows], oo_n), line.spot // 2)
        near = project_near(near, [[(g, "other")] for g in rest_n], 0, 7)

        near, back = lax.optimization_barrier((near, back))
        partials = all_tensor((near + back).astype(jnp.bfloat16))
        up_in, down_sum, bank = down_products(lengths, [sums, other], blocks)
    else:
        half = jnp.zeros((1,), jnp.int32)
        near_grads, far_grads = gather_any(output_grad, side, lane)
        far_gate = lax.ppermute(gate_preact, "dp", across)
        tile = width // split(width, max(1, width // 512), 128)
        up_in, down_sum, bank = down_products(
            lengths, all_tensor(local(tile)[0]), lax.all_gather(values, "dp", axis=0)
        )
        far = project([far_gate], [[(g, 0)] for g in far_grads], both, half, basis, zero, 0, tile)
        back = lax.ppermute(far, "dp", across)
        near = project([gate_preact], [[(g, 0)] for g in near_grads], both, half, basis, zero, 0, tile)
        partials = all_tensor((near + back).astype(jnp.bfloat16))

    return pl.pallas_call(
        score_kernel,
        in_specs=[pl.BlockSpec(memory_space=pltpu.SMEM)]
        + [pl.BlockSpec(memory_space=pltpu.VMEM)] * (3 + len(partials)),
        out_shape=jax.ShapeDtypeStruct((val_bank.shape[0], lengths.shape[1]), jnp.float32),
        compiler_params=pltpu.CompilerParams(vmem_limit_bytes=VMEM_BYTES),
    )(lengths, up_in, down_sum, bank, *partials).T


def solution(mesh):
    placed = (
        P(("parts", "dp"), "tensor"),
        P(("parts", "dp"), "tensor"),
        P(("parts", "dp"), "tensor"),
        P(("parts", "dp"), "tensor"),
        P("tensor", "dp"),
        P("tensor", None),
        P("tensor", None),
        P("tensor", None),
        P("tensor", None),
        P("tensor", "dp"),
        P(("parts", "dp"), None),
    )
    return jax.shard_map(
        body, mesh=mesh, in_specs=placed, out_specs=P(("parts", "dp"), "tensor"), check_vma=False
    )
```

```python
import functools

import jax
import jax.numpy as jnp
from jax import lax
from jax.experimental import pallas as pl
from jax.experimental.pallas import tpu as pltpu
from jax.sharding import PartitionSpec as P

R = 64
EPS = 1e-06
AXES = ("dp", "tensor")
NT = (((1,), (1,)), ((), ()))
VMEM_BYTES = 50 * 1024 * 1024


def after(value, *others):
    return lax.optimization_barrier((value,) + others)[0]


def silu(gate):
    return 0.5 * gate * (1.0 + jnp.tanh(0.5 * gate))


def project_kernel(bounds, parts, _, *refs):
    pieces = len(bounds) - 1
    gates = refs[:pieces]
    grads = refs[pieces : pieces + parts]
    weights = refs[pieces + parts : pieces + 2 * parts]
    basis, before, out, act = refs[pieces + 2 * parts :]
    step = pl.program_id(0)

    @pl.when(step == 0)
    def _():
        out[...] = before[...]

    for index, gate in enumerate(gates):

        @pl.when((step >= bounds[index]) & (step < bounds[index + 1]))
        def _(gate=gate):
            act[...] = silu(gate[...].astype(jnp.float32))

    hidden_grad = sum(
        lax.dot_general(grad[...], weight[...], NT, preferred_element_type=jnp.float32)
        for grad, weight in zip(grads, weights, strict=True)
    )
    up_grad = (hidden_grad * act[...]).astype(jnp.bfloat16)
    out[...] += lax.dot_general(basis[...], up_grad, NT, preferred_element_type=jnp.float32)


def project(gates, grads, weights, half, basis, before, start, tile):
    gates = [gate if isinstance(gate, tuple) else (gate, 0, gate.shape[1]) for gate in gates]
    bounds = [0]
    for _, _, width in gates:
        bounds.append(bounds[-1] + width // tile)
    pairs = [(g, block, w) for w, group in zip(weights, grads, strict=True) for g, block in group]
    parts = len(pairs)
    rows, depth = pairs[0][0].shape
    first = start // tile
    whole = lambda i, _: (0, 0)

    def gate_spec(index):
        low, high, skip = bounds[index], bounds[index + 1], gates[index][1] // tile
        return pl.BlockSpec((rows, tile), lambda i, _: (0, skip + jnp.clip(i - low, 0, high - low - 1)))

    def weight_spec(block):
        if block is None:
            return pl.BlockSpec((tile, depth), lambda i, half: (first + i, half[0]))
        if block == "other":
            return pl.BlockSpec((tile, depth), lambda i, half: (first + i, 1 - half[0]))
        return pl.BlockSpec((tile, depth), lambda i, _: (first + i, block))

    return pl.pallas_call(
        functools.partial(project_kernel, bounds, parts),
        grid_spec=pltpu.PrefetchScalarGridSpec(
            num_scalar_prefetch=1,
            grid=(bounds[-1],),
            in_specs=[gate_spec(index) for index in range(len(gates))]
            + [pl.BlockSpec((rows, depth), whole)] * parts
            + [weight_spec(block) for _, block, _ in pairs]
            + [pl.BlockSpec((R, tile), lambda i, _: (0, first + i)), pl.BlockSpec((R, rows), whole)],
            out_specs=pl.BlockSpec((R, rows), whole),
            scratch_shapes=[pltpu.VMEM((rows, tile), jnp.float32)],
        ),
        out_shape=jax.ShapeDtypeStruct((R, rows), jnp.float32),
        compiler_params=pltpu.CompilerParams(vmem_limit_bytes=VMEM_BYTES),
        cost_estimate=pl.CostEstimate(flops=1, bytes_accessed=1, transcendentals=0),
    )(half, *[gate for gate, _, _ in gates], *[g for g, _, _ in pairs], *[w for _, _, w in pairs], basis, before)


def local_kernel(cuts, gate, up, grad, normed, hidden_basis, output_basis, normed_basis, out, *cut_gates):
    step = pl.program_id(0)

    @pl.when(step == 0)
    def _():
        out[:R] = lax.dot_general(output_basis[...], grad[...], NT, preferred_element_type=jnp.float32)
        out[R : 2 * R] = lax.dot_general(normed_basis[...], normed[...], NT, preferred_element_type=jnp.float32)
        out[2 * R :] = jnp.zeros((R, out.shape[1]), jnp.float32)

    value = gate[...].astype(jnp.float32)
    hidden = (silu(value) * up[...].astype(jnp.float32)).astype(jnp.bfloat16)
    out[2 * R :] += lax.dot_general(hidden_basis[...], hidden, NT, preferred_element_type=jnp.float32)
    for (low, high), piece in zip(cuts, cut_gates, strict=True):

        @pl.when((step >= low) & (step < high))
        def _(piece=piece):
            piece[...] = gate[...]


def local_products(gate, up, grad, normed, hidden_basis, output_basis, normed_basis, tile, cuts=()):
    rows, width = gate.shape
    whole = lambda i: (0, 0)

    def cut_spec(low, high):
        return pl.BlockSpec((rows, tile), lambda i: (0, jnp.clip(i - low, 0, high - low - 1)))

    return pl.pallas_call(
        functools.partial(local_kernel, cuts),
        grid=(width // tile,),
        in_specs=[
            pl.BlockSpec((rows, tile), lambda i: (0, i)),
            pl.BlockSpec((rows, tile), lambda i: (0, i)),
            pl.BlockSpec(grad.shape, whole),
            pl.BlockSpec(normed.shape, whole),
            pl.BlockSpec((R, tile), lambda i: (0, i)),
            pl.BlockSpec(output_basis.shape, whole),
            pl.BlockSpec(normed_basis.shape, whole),
        ],
        out_specs=[pl.BlockSpec((3 * R, rows), whole)] + [cut_spec(*cut) for cut in cuts],
        out_shape=[jax.ShapeDtypeStruct((3 * R, rows), jnp.float32)]
        + [jax.ShapeDtypeStruct((rows, (high - low) * tile), gate.dtype) for low, high in cuts],
        compiler_params=pltpu.CompilerParams(vmem_limit_bytes=VMEM_BYTES),
        cost_estimate=pl.CostEstimate(flops=1, bytes_accessed=1, transcendentals=0),
    )(gate, up, grad, normed, hidden_basis, output_basis, normed_basis)


def by_example(lengths, value):
    token = lax.broadcasted_iota(jnp.int32, value.shape, 1)
    begin, members = 0, []
    for e in range(lengths.shape[1]):
        end = begin + lengths[0, e]
        members.append(jnp.where((token >= begin) & (token < end), value, 0.0))
        begin = end
    return jnp.concatenate(members, axis=0)


def outer_sums(lengths, left, right):
    return lax.dot_general(
        by_example(lengths, left),
        right,
        NT,
        precision=lax.Precision.HIGH,
        preferred_element_type=jnp.float32,
    )


def down_kernel(lengths, *refs):
    parts, (blocks, up_in, down_sum, bank) = refs[:-4], refs[-4:]
    totals = sum(part[...] for part in parts)
    up_in[...] = totals[R : 2 * R]
    down_sum[...] = outer_sums(lengths, totals[:R], totals[2 * R :])
    count, _, block, _ = blocks.shape
    for n in range(count):
        bank[:, n * block : (n + 1) * block, :] = blocks[n].astype(jnp.float32)


def down_products(lengths, parts, blocks):
    examples = lengths.shape[1]
    count, values, block, _ = blocks.shape
    return pl.pallas_call(
        down_kernel,
        in_specs=[pl.BlockSpec(memory_space=pltpu.SMEM)] + [pl.BlockSpec(memory_space=pltpu.VMEM)] * (len(parts) + 1),
        out_shape=(
            jax.ShapeDtypeStruct((R, parts[0].shape[1]), jnp.float32),
            jax.ShapeDtypeStruct((examples * R, R), jnp.float32),
            jax.ShapeDtypeStruct((values, count * block, R), jnp.float32),
        ),
        compiler_params=pltpu.CompilerParams(vmem_limit_bytes=VMEM_BYTES),
        cost_estimate=pl.CostEstimate(flops=1, bytes_accessed=1, transcendentals=0),
    )(lengths, *parts, blocks)


def score_kernel(lengths, up_in, down_sum, bank, *refs):
    partials, out = refs[:-1], refs[-1]
    up_sum = outer_sums(lengths, sum(part[...].astype(jnp.float32) for part in partials), up_in[...])
    values, examples = out.shape
    columns = lax.broadcasted_iota(jnp.int32, out.shape, 1)
    scores = jnp.zeros(out.shape, jnp.float32)
    for e in range(examples):
        down, up = down_sum[e * R : (e + 1) * R], up_sum[e * R : (e + 1) * R]
        mean = jnp.sum(jnp.sum(down * down + up * up, axis=0, keepdims=True), axis=1, keepdims=True) / (2 * R * R)
        inverse = lax.rsqrt(mean + EPS)
        down = (down * inverse).astype(jnp.bfloat16).astype(jnp.float32)
        up = (up * inverse).astype(jnp.bfloat16).astype(jnp.float32)
        by_column = [
            jnp.sum(down * bank[v, :R] + up * bank[v, R:], axis=0, keepdims=True) for v in range(values)
        ]
        one = jnp.sum(jnp.concatenate(by_column, axis=0), axis=1, keepdims=True)
        scores = jnp.where(columns == e, one, scores)
    out[...] = scores * float(2 * R * R) ** (-0.5)


def split(total, most, unit):
    for count in range(most, 0, -1):
        if total % (count * unit) == 0:
            return count
    return 1


class Line:
    def __init__(self, side, lane, place):
        self.spot = jnp.where(side == 0, place, 3 - place)
        self.even = (side + lane) % 2

    @staticmethod
    def at(a, c, s):
        return (2 * a + c) * 4 + (s if a == 0 else 3 - s)

    def move(self, value, hops, other=False):
        pairs = [
            (self.at(1 - a if other else a, c, s), self.at(a, c, t)) for a in (0, 1) for c in (0, 1) for s, t in hops
        ]
        return lax.ppermute(value, AXES, pairs)

    def pair(self, value):
        return self.move(value, [(0, 1), (1, 0), (2, 3), (3, 2)])

    def middle(self, value):
        return self.move(value, [(1, 2), (2, 1)])

    def outward(self, value):
        return self.move(value, [(1, 0), (2, 3)])

    def by_block(self, first, second, parity):
        keep = parity == self.even
        return jnp.where(keep, first, second), jnp.where(keep, second, first)


def gather_any(grad, side, lane):
    count = lax.axis_size("dp")
    whole = lax.all_gather(grad, "tensor", axis=1, tiled=True)
    block = whole.shape[1] // count
    far = lax.ppermute(
        lax.dynamic_slice_in_dim(whole, (1 - side) * 2 * block, 2 * block, axis=1),
        "dp",
        [(i, i ^ 2) for i in range(count)],
    )
    near = lax.dynamic_slice_in_dim(whole, side * 2 * block, 2 * block, axis=1)
    return [
        (jnp.where(lane == 0, v[:, :block], v[:, block:]), jnp.where(lane == 0, v[:, block:], v[:, :block]))
        for v in (near, far)
    ]


def all_tensor(value):
    count = lax.axis_size("tensor")
    if count > 8:
        return [lax.psum(value.astype(jnp.float32), "tensor")]
    return [value] + [
        lax.ppermute(value, "tensor", [(i, (i + k) % count) for i in range(count)]) for k in range(1, count)
    ]


def body(
    gate_preact,
    up_output,
    normed_input,
    output_grad,
    down_weight,
    normed_basis,
    output_basis,
    hidden_basis,
    up_basis,
    val_bank,
    lengths,
):
    rows, width = gate_preact.shape
    index, place = lax.axis_index("dp"), lax.axis_index("tensor")
    side, lane = index // 2, index % 2
    count = lax.axis_size("dp")
    across = [(i, i ^ 2) for i in range(count)]
    beside = [(i, i ^ 1) for i in range(count)]

    def local(tile, cuts=()):
        return local_products(
            gate_preact, up_output, output_grad, normed_input, hidden_basis.T, output_basis.T, normed_basis.T, tile, cuts
        )

    values = val_bank.reshape(val_bank.shape[0], -1, R)
    basis = up_basis.T
    zero = jnp.zeros((R, rows), jnp.float32)
    sibling = lax.ppermute(down_weight, "dp", beside)
    both = (down_weight, sibling)

    if count == 4 and lax.axis_size("tensor") == 4 and width % (7 * 128) == 0:
        line = Line(side, lane, place)
        depth = output_grad.shape[1] // 2
        ga, gb = output_grad[:, :depth], output_grad[:, depth:]
        half = (line.spot // 2).astype(jnp.int32)[None]
        inner = (line.spot == 1) | (line.spot == 2)
        tile = width // 7

        def exchange(value, apart):
            return lax.ppermute(value, "tensor", [(i, i ^ apart) for i in range(4)])

        def project_far(far, sources, grads, start):
            return project(sources, grads, both, half, basis, far, start * tile, tile)

        def project_near(near, grads, start, end):
            gate = (gate_preact, start * tile, (end - start) * tile)
            return project([gate], grads, both, half, basis, near, start * tile, tile)

        blocks = lax.all_gather(values, "dp", axis=0)
        xb = line.move(gb, [(3, 2), (2, 3)], other=True)
        ns = line.move(gb, [(0, 2), (1, 3)])
        xa = line.move(ga, [(3, 0), (2, 1)], other=True)
        s0 = lax.ppermute(gate_preact[:, : 2 * tile], "dp", across)
        sums, t2, t3, t5 = local(tile, ((2, 3), (3, 5), (5, 7)))

        ns, xa, xb, sums, t2, t3, t5 = lax.optimization_barrier((ns, xa, xb, sums, t2, t3, t5))
        own = jnp.concatenate([jnp.where(line.spot < 2, ga, ns), jnp.where(line.spot < 2, xa, xb)], axis=0)
        e, m = line.pair(own), line.middle(own)
        s2 = lax.ppermute(t2, "dp", across)

        e, m, sibling, s0, s2, t3, blocks = lax.optimization_barrier((e, m, sibling, s0, s2, t3, blocks))
        both = (down_weight, sibling)
        mm, o = line.middle(e), line.outward(m)
        first_n = line.by_block(own[:rows], e[:rows], line.spot % 2)
        first_f = line.by_block(own[rows:], e[rows:], line.spot % 2)
        first_n, first_f = [[(g, None)] for g in first_n], [[(g, None)] for g in first_f]
        s3 = lax.ppermute(t3, "dp", across)
        near = project_near(zero, first_n, 0, 7)
        far = project_far(zero, [s0, s2], first_f, 0)

        mm, o, s3, near, far, sums, t5 = lax.optimization_barrier((mm, o, s3, near, far, sums, t5))
        oo_f = line.outward(mm[rows:])
        s5 = lax.ppermute(t5, "dp", across)
        paired = exchange(sums, 1)
        third = jnp.where(inner, m, o)
        far = project_far(far, [s3], first_f, 3)

        oo_f, far, third, rest = lax.optimization_barrier((oo_f, far, third, mm))
        oo_n = line.outward(rest[:rows])
        rest_f = line.by_block(third[rows:], jnp.where(inner, rest[rows:], oo_f), line.spot // 2)
        rest_f = [[(g, "other")] for g in rest_f]
        all_f = [a + b for a, b in zip(first_f, rest_f, strict=True)]
        far = project_far(far, [s0, s2, s3], rest_f, 0)
        far = project_far(far, [s5], all_f, 5)

        oo_n, far, paired, sums, near = lax.optimization_barrier((oo_n, far, paired, sums, near))
        back = lax.ppermute(far, "dp", across)
        sums = sums + paired
        other = exchange(sums, 2)
        rest_n = line.by_block(third[:rows], jnp.where(inner, rest[:rows], oo_n), line.spot // 2)
        near = project_near(near, [[(g, "other")] for g in rest_n], 0, 7)

        near, back = lax.optimization_barrier((near, back))
        partials = all_tensor((near + back).astype(jnp.bfloat16))
        up_in, down_sum, bank = down_products(lengths, [sums, other], blocks)
    else:
        half = jnp.zeros((1,), jnp.int32)
        near_grads, far_grads = gather_any(output_grad, side, lane)
        far_gate = lax.ppermute(gate_preact, "dp", across)
        tile = width // split(width, max(1, width // 512), 128)
        up_in, down_sum, bank = down_products(
            lengths, all_tensor(local(tile)[0]), lax.all_gather(values, "dp", axis=0)
        )
        far = project([far_gate], [[(g, 0)] for g in far_grads], both, half, basis, zero, 0, tile)
        back = lax.ppermute(far, "dp", across)
        near = project([gate_preact], [[(g, 0)] for g in near_grads], both, half, basis, zero, 0, tile)
        partials = all_tensor((near + back).astype(jnp.bfloat16))

    return pl.pallas_call(
        score_kernel,
        in_specs=[pl.BlockSpec(memory_space=pltpu.SMEM)]
        + [pl.BlockSpec(memory_space=pltpu.VMEM)] * (3 + len(partials)),
        out_shape=jax.ShapeDtypeStruct((val_bank.shape[0], lengths.shape[1]), jnp.float32),
        compiler_params=pltpu.CompilerParams(vmem_limit_bytes=VMEM_BYTES),
    )(lengths, up_in, down_sum, bank, *partials).T


def solution(mesh):
    placed = (
        P(("parts", "dp"), "tensor"),
        P(("parts", "dp"), "tensor"),
        P(("parts", "dp"), "tensor"),
        P(("parts", "dp"), "tensor"),
        P("tensor", "dp"),
        P("tensor", None),
        P("tensor", None),
        P("tensor", None),
        P("tensor", None),
        P("tensor", "dp"),
        P(("parts", "dp"), None),
    )
    return jax.shard_map(
        body, mesh=mesh, in_specs=placed, out_specs=P(("parts", "dp"), "tensor"), check_vma=False
    )
```
